32 devices in a mesh: gz: 32 (over z, y, x, core).
Axes of the slice: x: 2, y: 2, z: 4, core: 2. Of those that a mesh axis runs over, the one named last changes fastest.
Arguments:
- moments: float32 [10, 256, 128, 128], P(None, 'gz')
- shapes: float32 [256, 3, 289], P('gz'), may hold values from -0.6 to 0.6
- anchors: int32 [256, 3], P('gz'), may hold values from 0 to 255, as said below
- synthesis: float32 [512, 289], replicated, may hold values from -6 to 6
- spreading: float32 [512, 2048], replicated, may hold values from 0 to 0.001953125
Outputs:
- moments_out: float32 [10, 256, 128, 128], P(None, 'gz')
- shapes_out: float32 [256, 3, 289], P('gz')
The draws below stay inside these ranges and needn't reach their ends.
Inputs may be any that keep to these rules, and one draw needn't show every extreme that they name: `anchors`: membrane m is owned by device m // 8; the slab of its box's first plane (anchor_z // 8) is its owner's, the one before or the one after, cyclically over 256 planes. Rows and columns lie below 128.
All inputs are finite; a program needn't handle non-finite values.
Results may differ from the reference program's by a relative error of at most 0.00017.
Values sent between devices are 32-bit elements; how exact they have to be, the bound alone decides.
A program may use at most 256 MiB of HBM per device.

```python
import jax
import jax.numpy as jnp
from jax import lax

PL = 8
NYX = 128
MEM_DEV = 8
LMAX = 16
NPTS = 512
BZ = 8
BXY = 16
STEPS = 3
NCOEF = 289
NZ = 256
MEMBRANES = 256


COMPONENT_PAIRS = ((0, 0), (1, 1), (2, 2), (0, 1), (0, 2), (1, 2))


def draw_moments(key, part):
    keys = jax.random.split(key, 3)
    grid = (NZ, NYX, NYX)
    density = 1.0 + 0.02 * jax.random.normal(keys[0], grid, jnp.float32)
    momentum = 0.04 * jax.random.normal(keys[1], (3,) + grid, jnp.float32)
    noise = 0.01 * jax.random.normal(keys[2], (6,) + grid, jnp.float32)
    seconds = []
    for position, (axis_a, axis_b) in enumerate(COMPONENT_PAIRS):
        current = momentum[axis_a] * momentum[axis_b] + noise[position]
        if axis_a == axis_b:
            current = current + density / 3.0
        seconds.append(current)
    return jnp.concatenate([density[None], momentum, jnp.stack(seconds)], axis=0)


def draw_anchors(key, part):
    keys = jax.random.split(key, 4)
    owners = jnp.arange(MEMBRANES, dtype=jnp.int32) // MEM_DEV
    drift = jax.random.randint(keys[0], (MEMBRANES,), -1, 2, dtype=jnp.int32)
    inside = jax.random.randint(keys[1], (MEMBRANES,), 0, PL, dtype=jnp.int32)
    plane_first = ((owners + drift) * PL + inside) % NZ
    plane_first = plane_first.at[MEMBRANES - 1].set(NZ - 1)
    row_first = jax.random.randint(keys[2], (MEMBRANES,), 0, NYX, dtype=jnp.int32)
    row_first = row_first.at[0].set(0)
    column_first = jax.random.randint(keys[3], (MEMBRANES,), 0, NYX, dtype=jnp.int32)
    return jnp.stack([plane_first, row_first, column_first], axis=1)


def block_levels(stream_key, shape, cuts, low, largest):
    level = 1.0
    for dim, shards_of in cuts:
        steps = jax.random.uniform(jax.random.fold_in(jax.random.fold_in(stream_key, 6), dim), (shards_of,), jnp.float32, low / len(cuts), largest / len(cuts))
        level = level * jnp.repeat(jnp.exp(steps), shape[dim] // shards_of).reshape((-1,) + (1,) * (len(shape) - 1 - dim))
    return level


def scatter_about(key, extent, scale, limit, shards=(), kind=jnp.bfloat16):
    values = scale * jax.random.normal(key, extent, jnp.float32)
    if shards:
        values = values * block_levels(key, extent, shards, -0.22, 0.18)
    return jnp.clip(values, -limit, limit).astype(kind)


def setup_inputs(seed: int = 0) -> dict:
    splits = jax.random.split(jax.random.key(seed), 6)
    return {
        "moments": draw_moments(jax.random.fold_in(splits[5], 71), 0),
        "shapes": scatter_about(splits[1], (MEMBRANES, 3, NCOEF), 0.1, 0.6, ((0, 32),), jnp.float32),
        "anchors": draw_anchors(jax.random.fold_in(splits[5], 71), 0),
        "synthesis": scatter_about(splits[3], (NPTS, NCOEF), 1.0, 6.0, (), jnp.float32),
        "spreading": jnp.clip(jax.random.uniform(splits[4], (NPTS, BZ * BXY * BXY), jnp.float32, 0.0, 0.001953125), 0.0, 0.001953125),
    }


RELAX_RATE = 1.25
STIFF_SCALE = 0.002
MOBILITY = 0.5
PRECISE = lax.Precision.HIGHEST
COMPONENT_PAIRS = ((0, 0), (1, 1), (2, 2), (0, 1), (0, 2), (1, 2))


def lattice_links():
    links = []
    for along_z in (-1, 0, 1):
        for along_y in (-1, 0, 1):
            for along_x in (-1, 0, 1):
                links.append((along_z, along_y, along_x))
    return links


def link_weight(link):
    length = abs(link[0]) + abs(link[1]) + abs(link[2])
    return (8.0 / 27.0, 2.0 / 27.0, 1.0 / 54.0, 1.0 / 216.0)[length]


def rebuild_table():
    table_rows = []
    for link in lattice_links():
        weight = link_weight(link)
        squared = link[0] * link[0] + link[1] * link[1] + link[2] * link[2]
        entries = [weight * (1.0 - 1.5 * (squared - 1.0))]
        entries += [3.0 * weight * link[axis_a] for axis_a in range(3)]
        for axis_a, axis_b in COMPONENT_PAIRS:
            if axis_a == axis_b:
                entries.append(4.5 * weight * (link[axis_a] * link[axis_a] - 1.0 / 3.0))
            else:
                entries.append(9.0 * weight * link[axis_a] * link[axis_b])
        table_rows.append(entries)
    return jnp.asarray(table_rows, dtype=jnp.float32)


def moment_table():
    links = lattice_links()
    table_rows = [[1.0 for link in links]]
    for axis_a in range(3):
        table_rows.append([float(link[axis_a]) for link in links])
    for axis_a, axis_b in COMPONENT_PAIRS:
        table_rows.append([float(link[axis_a] * link[axis_b]) for link in links])
    return jnp.asarray(table_rows, dtype=jnp.float32)


def degree_stiffness(coefficient_count):
    numbers = jnp.arange(coefficient_count, dtype=jnp.int32)
    degree = jnp.zeros((coefficient_count,), jnp.int32)
    for degree_step in range(1, LMAX + 1):
        degree = degree + (numbers >= degree_step * degree_step).astype(jnp.int32)
    return STIFF_SCALE * (degree * (degree + 1) + 2).astype(jnp.float32)


def collide(moments, force_field):
    density = moments[0]
    momentum = moments[1:4]
    velocity = momentum + 0.5 * force_field
    seconds = []
    for position, (axis_a, axis_b) in enumerate(COMPONENT_PAIRS):
        current = moments[4 + position]
        target = velocity[axis_a] * velocity[axis_b]
        if axis_a == axis_b:
            target = target + density / 3.0
        source = force_field[axis_a] * velocity[axis_b] + velocity[axis_a] * force_field[axis_b]
        seconds.append(current + RELAX_RATE * (target - current) + (1.0 - 0.5 * RELAX_RATE) * source)
    return jnp.concatenate([density[None], momentum + force_field, jnp.stack(seconds)], axis=0)


def stream_planes(extended, planes):
    distributions = jnp.einsum('qm,mzyx->qzyx', rebuild_table(), extended, precision=PRECISE)
    moved = []
    for q_index, link in enumerate(lattice_links()):
        source = distributions[q_index, 1 - link[0]:1 - link[0] + planes]
        moved.append(jnp.roll(source, (link[1], link[2]), axis=(1, 2)))
    return jnp.einsum('mq,qzyx->mzyx', moment_table(), jnp.stack(moved), precision=PRECISE)


def reference(moments, shapes, anchors, synthesis, spreading):
    total_planes = moments.shape[1]
    side_cells = moments.shape[2]
    block_count = total_planes // PL
    membranes = shapes.shape[0]
    stiffness = degree_stiffness(shapes.shape[2])
    box_depth = jnp.arange(BZ, dtype=jnp.int32)
    across = jnp.arange(BXY, dtype=jnp.int32)
    plane_ids = (anchors[:, 0:1] + box_depth[None, :]) % total_planes
    row_ids = (anchors[:, 1:2] + across[None, :]) % side_cells
    column_ids = (anchors[:, 2:3] + across[None, :]) % side_cells

    def add_box(force_sum, pieces):
        one_box, planes_at, rows_at, columns_at = pieces
        force_sum = force_sum.at[:, planes_at[:, None, None], rows_at[None, :, None], columns_at[None, None, :]].add(one_box)
        return force_sum, None

    for iteration in range(STEPS):
        coefs = -stiffness * shapes
        surface = jnp.einsum('mcn,pn->mcp', coefs, synthesis, precision=PRECISE)
        boxes = jnp.einsum('mcp,pq->mcq', surface, spreading, precision=PRECISE).reshape(membranes, 3, BZ, BXY, BXY)
        empty_field = jnp.zeros((3, total_planes, side_cells, side_cells), jnp.float32)
        force_field, unused = lax.scan(add_box, empty_field, (boxes, plane_ids, row_ids, column_ids))
        post = collide(moments, force_field)
        padded = jnp.concatenate([post[:, -1:], post, post[:, :1]], axis=1)

        def one_block(first_plane):
            return stream_planes(lax.dynamic_slice_in_dim(padded, first_plane, PL + 2, 1), PL)

        blocks = lax.map(one_block, jnp.arange(block_count, dtype=jnp.int32) * PL)
        moments = jnp.transpose(blocks, (1, 0, 2, 3, 4)).reshape(10, total_planes, side_cells, side_cells)
        velocity = moments[1:4]
        sampled = velocity[:, plane_ids[:, :, None, None], row_ids[:, None, :, None], column_ids[:, None, None, :]]
        sampled = jnp.transpose(sampled, (1, 0, 2, 3, 4)).reshape(membranes, 3, BZ * BXY * BXY)
        surface_speed = jnp.einsum('mcq,pq->mcp', sampled, spreading, precision=PRECISE)
        shapes = shapes + MOBILITY * jnp.einsum('mcp,pn->mcn', surface_speed, synthesis, precision=PRECISE)
    return moments, shapes
```

```python
import jax
import jax.numpy as jnp
from jax import lax
from jax.experimental import pallas as pl
from jax.experimental.pallas import tpu as pltpu
from jax.sharding import PartitionSpec as P

LMAX = 16
BZ = 8
BXY = 16
STEPS = 3

RELAX_RATE = 1.25
STIFF_SCALE = 0.002
MOBILITY = 0.5
GROUPS = 4
ROWS = 8
NN = (((1,), (0,)), ((), ()))
NT = (((1,), (1,)), ((), ()))
VMEM_LIMIT = 48 * 1024 * 1024


def shifted(block, distance):
    count = lax.axis_size("gz")
    return lax.ppermute(block, "gz", [((i - distance) % count, i) for i in range(count)])


def degree_stiffness(coefficient_count):
    numbers = jnp.arange(coefficient_count, dtype=jnp.int32)
    degree = jnp.zeros((coefficient_count,), jnp.int32)
    for degree_step in range(1, LMAX + 1):
        degree = degree + (numbers >= degree_step * degree_step).astype(jnp.int32)
    return STIFF_SCALE * (degree * (degree + 1) + 2).astype(jnp.float32)


def halves(value):
    high = value.astype(jnp.bfloat16)
    low = (value - high.astype(jnp.float32)).astype(jnp.bfloat16)
    return high, low


def dot(a, b, dims):
    return lax.dot_general(a, b, dims, preferred_element_type=jnp.float32)


def dot_split(value, high, low, dims):
    value_high, value_low = halves(value)
    return dot(value_high, high, dims) + (dot(value_low, high, dims) + dot(value_high, low, dims))


def prepare_kernel(spreading_ref, high_ref, low_ref):
    lanes = BZ * BXY
    row_count = spreading_ref.shape[0]
    unit = lax.broadcasted_iota(jnp.int32, (16, lanes), 1) // BXY

    def chunk(index, carry):
        rows = pl.ds(pl.multiple_of(index * 16, 16), 16)
        for half in range(BXY // BZ):
            tiles = [
                spreading_ref[rows, pl.ds((k * (BXY // BZ) + half) * lanes, lanes)]
                for k in range(BZ)
            ]
            distance = 1
            while distance < BZ:
                upper = (unit & distance) != 0
                for a in range(BZ):
                    if a & distance == 0:
                        b = a + distance
                        left = jnp.where(upper, pltpu.roll(tiles[b], distance * BXY, 1), tiles[a])
                        right = jnp.where(
                            upper, tiles[b], pltpu.roll(tiles[a], lanes - distance * BXY, 1)
                        )
                        tiles[a], tiles[b] = left, right
                distance *= 2
            for position in range(BZ):
                high, low = halves(tiles[position])
                columns = pl.ds((half * BZ + position) * lanes, lanes)
                high_ref[rows, columns] = high
                low_ref[rows, columns] = low
        return carry

    lax.fori_loop(0, row_count // 16, chunk, 0)


def plane_range(first, planes):
    return jnp.maximum(first, 0), jnp.minimum(first + BZ, planes)


def force_kernel(
    started, place_ref, moments_ref, shapes_ref, own_ref, below_ref, above_ref, stiffness_ref,
    synth_high, synth_low, spread_high, spread_low,
    post_ref, up_ref, down_ref, shapes_out, boxes_ref, force_ref,
):
    planes, side, lanes = moments_ref.shape[1:]
    rows = shapes_ref.shape[0]
    slots = rows // 3
    shared = below_ref.shape[0]
    force_ref[...] = jnp.zeros_like(force_ref)
    if started:
        shapes_out[...] = shapes_ref[...] + MOBILITY * own_ref[...]
        shapes_out[0:shared, :] += MOBILITY * below_ref[...]
        shapes_out[rows - shared :, :] += MOBILITY * above_ref[...]
    else:
        shapes_out[...] = shapes_ref[...]
    coefs = -stiffness_ref[...] * shapes_out[...]
    surface = dot_split(coefs, synth_high[...], synth_low[...], NT)
    boxes = dot_split(surface, spread_high[...], spread_low[...], NN)
    for i in range(BXY):
        boxes_ref[i * rows : (i + 1) * rows, :] = boxes[:, i * lanes : (i + 1) * lanes]
    lane = lax.broadcasted_iota(jnp.int32, (BXY, lanes), 1)

    def slot(s, carry):
        first, row, column = place_ref[s, 0], place_ref[s, 1], place_ref[s, 2]
        low, high = plane_range(first, planes)

        @pl.when(low < high)
        def _():
            window = ((lane - column) & (lanes - 1)) < BXY
            tiles = [boxes_ref[pl.ds(s * 3 + c, BXY, stride=rows), :] for c in range(3)]

            def plane(z, inner):
                turn = (column - BXY * (z - first)) & (lanes - 1)
                for c in range(3):
                    moved = jnp.where(window, pltpu.roll(tiles[c], turn, 1), 0.0)
                    force_ref[c, z, pl.ds(row, BXY), :] += moved
                return inner

            lax.fori_loop(low, high, plane, 0)

        return carry

    lax.fori_loop(0, slots, slot, 0)
    for c in range(3):
        force_ref[c, :, 0:BXY, :] += force_ref[c, :, side : side + BXY, :]

    def collide(index, carry):
        z = index // (side // ROWS)
        at = pl.ds(pl.multiple_of((index % (side // ROWS)) * ROWS, ROWS), ROWS)
        rho, jz, jy, jx, zz, yy, xx, zy, zx, yx = [moments_ref[n, z, at, :] for n in range(10)]
        fz, fy, fx = [force_ref[c, z, at, :] for c in range(3)]
        uz, uy, ux = jz + 0.5 * fz, jy + 0.5 * fy, jx + 0.5 * fx
        third = rho * (1.0 / 3.0)
        half_source = 1.0 - 0.5 * RELAX_RATE

        def second(current, target, source):
            return current + RELAX_RATE * (target - current) + half_source * source

        zz = second(zz, uz * uz + third, 2.0 * (fz * uz))
        yy = second(yy, uy * uy + third, 2.0 * (fy * uy))
        xx = second(xx, ux * ux + third, 2.0 * (fx * ux))
        zy = second(zy, uz * uy, fz * uy + uz * fy)
        zx = second(zx, uz * ux, fz * ux + uz * fx)
        yx = second(yx, uy * ux, fy * ux + uy * fx)
        jz, jy, jx = 0.5 * (jz + fz), (jy + fy) * (1.0 / 6.0), (jx + fx) * (1.0 / 6.0)
        zz_half, zy, zx = 0.5 * zz, 0.5 * zy, 0.5 * zx
        fields = (
            zz_half + jz, jy + zy, jx + zx,
            (yy - third) * (1.0 / 6.0), (xx - third) * (1.0 / 6.0), yx * (1.0 / 6.0),
            zz_half - jz, jy - zy, jx - zx,
            rho - zz,
        )
        for n in range(10):
            post_ref[n, z, at, :] = fields[n]
        return carry

    lax.fori_loop(0, planes * (side // ROWS), collide, 0, unroll=2)
    up_ref[...] = post_ref[0:6, planes - 1]
    down_ref[...] = post_ref[3:9, 0]


def hermite_split(a0, a1, a2):
    base = a0 * (1.0 / 6.0)
    if a2 is not None:
        base = base + 0.5 * a2
    rest = a0 * (2.0 / 3.0)
    if a2 is not None:
        rest = rest - a2
    if a1 is None:
        return base, rest, base
    odd = 0.5 * a1
    return base + odd, rest, base - odd


Y_GROUPS = ((0, 0), (1, 0), (0, 1), (2, 0), (0, 2), (1, 1))
Y_TARGETS = ((0, 2, 5), (1, 7), (3, 9), (4,), (6,), (8,))


def stream_kernel(
    last, place_ref, post_ref, below_ref, above_ref, shapes_ref, home_ref,
    synth_high, synth_low, spread_high, spread_low,
    moments_ref, partial_ref, mixed_ref, speed_ref, sampled_ref,
):
    planes, side, lanes = post_ref.shape[1:]
    rows = shapes_ref.shape[0]
    slots = rows // 3
    for z in range(planes):

        def mix(index, carry, z=z):
            at = pl.ds(pl.multiple_of(index * ROWS, ROWS), ROWS)
            if z == 0:
                rising = [below_ref[n, at, :] for n in range(6)]
            else:
                rising = [post_ref[n, z - 1, at, :] for n in range(6)]
            if z == planes - 1:
                falling = [above_ref[n, at, :] for n in (3, 4, 5, 0, 1, 2)]
            else:
                falling = [post_ref[n, z + 1, at, :] for n in (6, 7, 8, 3, 4, 5)]
            here = [post_ref[n, z, at, :] for n in range(10)]
            rest = [
                here[9], 2.0 * (here[1] + here[7]), 2.0 * (here[2] + here[8]),
                4.0 * here[3], 4.0 * here[4], 4.0 * here[5],
            ]
            along_z = []
            for g in range(6):
                total = rising[g] + falling[g]
                along_z.append((total + rest[g], rising[g] - falling[g], total))
            for mz in range(3):
                one, in_y, in_x, in_yy, in_xx, in_yx = [along_z[g][mz] for g in range(6)]
                along_x = []
                for a0, a1, a2 in ((one, in_x, in_xx), (in_y, in_yx, None), (in_yy, None, None)):
                    right, stay, left = hermite_split(a0, a1, a2)
                    right = pltpu.roll(right, 1, 1)
                    left = pltpu.roll(left, lanes - 1, 1)
                    total = right + left
                    along_x.append((total + stay, right - left, total))
                for mx in range(3 - mz):
                    group = Y_GROUPS.index((mz, mx))
                    parts = hermite_split(along_x[0][mx], along_x[1][mx], along_x[2][mx])
                    for n in range(3):
                        mixed_ref[group * 3 + n, at, :] = parts[n]
            return carry

        lax.fori_loop(0, side // ROWS, mix, 0, unroll=2)
        for group, targets in enumerate(Y_TARGETS):
            up = pltpu.roll(mixed_ref[group * 3], 1, 0)
            down = pltpu.roll(mixed_ref[group * 3 + 2], side - 1, 0)
            total = up + down
            results = (total + mixed_ref[group * 3 + 1], up - down, total)
            for my, target in enumerate(targets):
                moments_ref[target, z] = results[my]
                if 1 <= target <= 3:
                    speed_ref[target - 1, z, 0:side, :] = results[my]
                    speed_ref[target - 1, z, side : side + BXY, :] = results[my][0:BXY, :]

    unit = lax.broadcasted_iota(jnp.int32, (BXY, lanes), 1) // BXY

    def slot(s, carry):
        first, row, column = place_ref[s, 0], place_ref[s, 1], place_ref[s, 2]
        low, high = plane_range(first, planes)

        def plane(z, tiles):
            k = z - first
            turn = (BXY * k - column) & (lanes - 1)
            return tuple(
                jnp.where(unit == k, pltpu.roll(speed_ref[c, z, pl.ds(row, BXY), :], turn, 1), tiles[c])
                for c in range(3)
            )

        empty = jnp.zeros((BXY, lanes), jnp.float32)
        tiles = lax.fori_loop(low, high, plane, (empty, empty, empty))
        for c in range(3):
            sampled_ref[pl.ds(s * 3 + c, BXY, stride=rows), :] = tiles[c]
        return carry

    lax.fori_loop(0, slots, slot, 0)
    sampled = jnp.concatenate(
        [sampled_ref[i * rows : (i + 1) * rows, :] for i in range(BXY)], axis=1
    )
    surface = dot_split(sampled, spread_high[...], spread_low[...], NT)
    partial = dot_split(surface, synth_high[...], synth_low[...], NN)
    if not last:
        partial_ref[...] = partial
    else:
        partial_ref[...] = MOBILITY * partial + jnp.where(home_ref[...] > 0, shapes_ref[...], 0.0)


def per_device(moments, shapes, anchors, synthesis, spreading):
    planes, side, lanes = moments.shape[1:]
    total_planes = planes * lax.axis_size("gz")
    first_plane = lax.axis_index("gz") * planes
    owned, parts, count = shapes.shape
    points = synthesis.shape[0]
    wide = -(-count // 128) * 128
    slots = GROUPS * owned
    rows = slots * parts
    shared = rows - owned * parts
    vmem = pl.BlockSpec(memory_space=pltpu.VMEM)
    smem = pl.BlockSpec(memory_space=pltpu.SMEM)
    params = pltpu.CompilerParams(vmem_limit_bytes=VMEM_LIMIT)

    def struct(*shape, dtype=jnp.float32):
        return jax.ShapeDtypeStruct(shape, dtype)

    stiffness = jnp.pad(degree_stiffness(count), (0, wide - count))[None]
    flat = jnp.pad(shapes.reshape(owned * parts, count), ((0, 0), (0, wide - count)))
    held = jnp.concatenate([shifted(flat, 2), shifted(flat, 1), flat, shifted(flat, -1)], axis=0)
    place = jnp.concatenate(
        [shifted(anchors, 2), shifted(anchors, 1), anchors, shifted(anchors, -1)], axis=0
    )
    ahead = jnp.mod(place[:, 0] - first_plane, total_planes)
    ahead = jnp.where(ahead > total_planes - BZ, ahead - total_planes, ahead)
    home = ((ahead >= 0) & (ahead < planes)).astype(jnp.int32)
    home = jnp.broadcast_to(home[:, None, None], (slots, parts, wide)).reshape(rows, wide)
    place = jnp.stack([ahead, place[:, 1], place[:, 2]], axis=1)

    synth = jnp.pad(synthesis, ((0, 0), (0, wide - count)))
    synth_high = lax.reduce_precision(synth, 8, 7)
    synth_low = (synth - synth_high).astype(jnp.bfloat16)
    synth_high = synth_high.astype(jnp.bfloat16)
    spread_high, spread_low = pl.pallas_call(
        prepare_kernel,
        out_shape=[struct(points, spreading.shape[1], dtype=jnp.bfloat16)] * 2,
        in_specs=[vmem],
        out_specs=[vmem, vmem],
        compiler_params=params,
        name="prepare",
    )(spreading)
    tables = (synth_high, synth_low, spread_high, spread_low)

    own = jnp.zeros((rows, wide), jnp.float32)
    below = above = jnp.zeros((shared, wide), jnp.float32)
    for iteration in range(STEPS):

        def force_body(*refs, started=iteration > 0):
            force_kernel(started, *refs)

        post, up, down, held = pl.pallas_call(
            force_body,
            out_shape=[
                struct(10, planes, side, lanes),
                struct(6, side, lanes),
                struct(6, side, lanes),
                struct(rows, wide),
            ],
            in_specs=[smem] + [vmem] * 10,
            out_specs=[vmem] * 4,
            scratch_shapes=[
                pltpu.VMEM((BXY * rows, lanes), jnp.float32),
                pltpu.VMEM((3, planes, side + BXY, lanes), jnp.float32),
            ],
            compiler_params=params,
            name="collide",
        )(place, moments, held, own, below, above, stiffness, *tables)
        from_below = shifted(up, 1)
        from_above = shifted(down, -1)

        def stream_body(*refs, last=iteration == STEPS - 1):
            stream_kernel(last, *refs)

        moments, own = pl.pallas_call(
            stream_body,
            out_shape=[struct(10, planes, side, lanes), struct(rows, wide)],
            in_specs=[smem] + [vmem] * 9,
            out_specs=[vmem] * 2,
            scratch_shapes=[
                pltpu.VMEM((18, side, lanes), jnp.float32),
                pltpu.VMEM((3, planes, side + BXY, lanes), jnp.float32),
                pltpu.VMEM((BXY * rows, lanes), jnp.float32),
            ],
            compiler_params=params,
            name="stream",
        )(place, post, from_below, from_above, held, home, *tables)
        if iteration < STEPS - 1:
            below = shifted(own[rows - shared :], 1)
            above = shifted(own[:shared], -1)
    groups = own.reshape(GROUPS, owned * parts, wide)
    result = groups[2] + shifted(groups[3], 1) + shifted(groups[1], -1) + shifted(groups[0], -2)
    return moments, result[:, :count].reshape(owned, parts, count)


def solution(mesh):
    return jax.shard_map(
        per_device,
        mesh=mesh,
        in_specs=(P(None, "gz", None, None), P("gz", None, None), P("gz", None), P(), P()),
        out_specs=(P(None, "gz", None, None), P("gz", None, None)),
        check_vma=False,
    )
```

```python
import jax
import jax.numpy as jnp
from jax import lax
from jax.experimental import pallas as pl
from jax.experimental.pallas import tpu as pltpu
from jax.sharding import PartitionSpec as P

LMAX = 16
BZ = 8
BXY = 16
STEPS = 3

RELAX_RATE = 1.25
STIFF_SCALE = 0.002
MOBILITY = 0.5
GROUPS = 4
ROWS = 8
NN = (((1,), (0,)), ((), ()))
NT = (((1,), (1,)), ((), ()))
VMEM_LIMIT = 48 * 1024 * 1024


def shifted(block, distance):
    count = lax.axis_size("gz")
    return lax.ppermute(block, "gz", [((i - distance) % count, i) for i in range(count)])


def degree_stiffness(coefficient_count):
    numbers = jnp.arange(coefficient_count, dtype=jnp.int32)
    degree = jnp.zeros((coefficient_count,), jnp.int32)
    for degree_step in range(1, LMAX + 1):
        degree = degree + (numbers >= degree_step * degree_step).astype(jnp.int32)
    return STIFF_SCALE * (degree * (degree + 1) + 2).astype(jnp.float32)


def halves(value):
    high = value.astype(jnp.bfloat16)
    low = (value - high.astype(jnp.float32)).astype(jnp.bfloat16)
    return high, low


def dot(a, b, dims):
    return lax.dot_general(a, b, dims, preferred_element_type=jnp.float32)


def dot_split(value, high, low, dims):
    value_high, value_low = halves(value)
    return dot(value_high, high, dims) + (dot(value_low, high, dims) + dot(value_high, low, dims))


def prepare_kernel(spreading_ref, high_ref, low_ref):
    lanes = BZ * BXY
    row_count = spreading_ref.shape[0]
    unit = lax.broadcasted_iota(jnp.int32, (16, lanes), 1) // BXY

    def chunk(index, carry):
        rows = pl.ds(pl.multiple_of(index * 16, 16), 16)
        for half in range(BXY // BZ):
            tiles = [
                spreading_ref[rows, pl.ds((k * (BXY // BZ) + half) * lanes, lanes)]
                for k in range(BZ)
            ]
            distance = 1
            while distance < BZ:
                upper = (unit & distance) != 0
                for a in range(BZ):
                    if a & distance == 0:
                        b = a + distance
                        left = jnp.where(upper, pltpu.roll(tiles[b], distance * BXY, 1), tiles[a])
                        right = jnp.where(
                            upper, tiles[b], pltpu.roll(tiles[a], lanes - distance * BXY, 1)
                        )
                        tiles[a], tiles[b] = left, right
                distance *= 2
            for position in range(BZ):
                high, low = halves(tiles[position])
                columns = pl.ds((half * BZ + position) * lanes, lanes)
                high_ref[rows, columns] = high
                low_ref[rows, columns] = low
        return carry

    lax.fori_loop(0, row_count // 16, chunk, 0)


def hermite_split(a0, a1, a2):
    base = a0 * (1.0 / 6.0)
    if a2 is not None:
        base = base + 0.5 * a2
    rest = a0 * (2.0 / 3.0)
    if a2 is not None:
        rest = rest - a2
    if a1 is None:
        return base, rest, base
    odd = 0.5 * a1
    return base + odd, rest, base - odd


Y_GROUPS = ((0, 0), (1, 0), (0, 1), (2, 0), (0, 2), (1, 1))
Y_TARGETS = ((0, 2, 5), (1, 7), (3, 9), (4,), (6,), (8,))


def collide_cell(moments, force):
    rho, jz, jy, jx, zz, yy, xx, zy, zx, yx = moments
    fz, fy, fx = force
    uz, uy, ux = jz + 0.5 * fz, jy + 0.5 * fy, jx + 0.5 * fx
    third = rho * (1.0 / 3.0)
    half_source = 1.0 - 0.5 * RELAX_RATE

    def second(current, target, source):
        return current + RELAX_RATE * (target - current) + half_source * source

    zz = second(zz, uz * uz + third, 2.0 * (fz * uz))
    yy = second(yy, uy * uy + third, 2.0 * (fy * uy))
    xx = second(xx, ux * ux + third, 2.0 * (fx * ux))
    zy = second(zy, uz * uy, fz * uy + uz * fy)
    zx = second(zx, uz * ux, fz * ux + uz * fx)
    yx = second(yx, uy * ux, fy * ux + uy * fx)
    jz, jy, jx = 0.5 * (jz + fz), (jy + fy) * (1.0 / 6.0), (jx + fx) * (1.0 / 6.0)
    zz_half, zy, zx = 0.5 * zz, 0.5 * zy, 0.5 * zx
    return (
        zz_half + jz, jy + zy, jx + zx,
        (yy - third) * (1.0 / 6.0), (xx - third) * (1.0 / 6.0), yx * (1.0 / 6.0),
        zz_half - jz, jy - zy, jx - zx,
        rho - zz,
    )


def mix_cell(rising, here, falling, lanes):
    rest = [
        here[9], 2.0 * (here[1] + here[7]), 2.0 * (here[2] + here[8]),
        4.0 * here[3], 4.0 * here[4], 4.0 * here[5],
    ]
    along_z = []
    for g in range(6):
        total = rising[g] + falling[g]
        along_z.append((total + rest[g], rising[g] - falling[g], total))
    mixed = [None] * 18
    for mz in range(3):
        one, in_y, in_x, in_yy, in_xx, in_yx = [along_z[g][mz] for g in range(6)]
        along_x = []
        for a0, a1, a2 in ((one, in_x, in_xx), (in_y, in_yx, None), (in_yy, None, None)):
            right, stay, left = hermite_split(a0, a1, a2)
            right = pltpu.roll(right, 1, 1)
            left = pltpu.roll(left, lanes - 1, 1)
            total = right + left
            along_x.append((total + stay, right - left, total))
        for mx in range(3 - mz):
            group = Y_GROUPS.index((mz, mx))
            parts = hermite_split(along_x[0][mx], along_x[1][mx], along_x[2][mx])
            for n in range(3):
                mixed[group * 3 + n] = parts[n]
    return mixed


def flow_kernel(
    devices, place_ref, moments_in, shapes_ref, home_ref, stiffness_ref,
    synth_high, synth_low, spread_high, spread_low,
    moments_out, shapes_out,
    moments_ref, post_ref, force_ref, speed_ref, mixed_ref, boxes_ref, spots_ref, rows_ref, held_ref,
    partial_ref, below_ref, above_ref, under_ref, over_ref, final_ref,
    local_sem, send_sem, recv_sem,
):
    planes, side, lanes = moments_ref.shape[1:]
    rows = shapes_ref.shape[0]
    slots = rows // 3
    block = rows // GROUPS
    shared = rows - block
    chunks = side // ROWS
    me = lax.axis_index("gz")
    after, before = lax.rem(me + 1, devices), lax.rem(me + devices - 1, devices)
    second_after, second_before = lax.rem(me + 2, devices), lax.rem(me + devices - 2, devices)

    load = pltpu.make_async_copy(moments_in, moments_ref, local_sem.at[0])
    load.start()
    barrier = pltpu.get_barrier_semaphore()
    for other in (before, after, second_before, second_after):
        pl.semaphore_signal(
            barrier, inc=1, device_id=(other,), device_id_type=pl.DeviceIdType.MESH
        )
    pl.semaphore_wait(barrier, 4)

    def remote(source, target, number, device):
        return pltpu.make_async_remote_copy(
            src_ref=source, dst_ref=target, send_sem=send_sem.at[number],
            recv_sem=recv_sem.at[number], device_id=(device,),
            device_id_type=pl.DeviceIdType.MESH,
        )

    lane = lax.broadcasted_iota(jnp.int32, (BXY, lanes), 1)
    depth = lax.broadcasted_iota(jnp.int32, (BXY, lanes), 0)
    unit = lane // BXY

    def spot(s, carry):
        hit = ((lane - place_ref[s, 1] - depth) & (side - 1)) == 0
        boxes_ref[pl.ds(pl.multiple_of(s * BXY, BXY), BXY), :] = jnp.where(hit, 1.0, 0.0)
        return carry

    lax.fori_loop(0, slots, spot, 0)
    spots = boxes_ref[0 : slots * BXY, :].T.astype(jnp.bfloat16)
    spots_ref[:, 0 : slots * BXY] = spots
    spots_ref[:, slots * BXY :] = spots
    held_ref[...] = shapes_ref[...]

    def collide_plane(z):
        def chunk(index, carry):
            at = pl.ds(pl.multiple_of(index * ROWS, ROWS), ROWS)
            fields = collide_cell(
                [moments_ref[n, z, at, :] for n in range(10)],
                [force_ref[c, z, at, :] for c in range(3)],
            )
            for n in range(10):
                post_ref[n, z, at, :] = fields[n]
            return carry

        lax.fori_loop(0, chunks, chunk, 0, unroll=2)

    def stream_plane(z, rising, falling):
        def chunk(index, carry):
            at = pl.ds(pl.multiple_of(index * ROWS, ROWS), ROWS)
            here = [post_ref[n, z, at, :] for n in range(10)]
            mixed = mix_cell(rising(at), here, falling(at), lanes)
            for n in range(18):
                mixed_ref[n, at, :] = mixed[n]
            return carry

        lax.fori_loop(0, chunks, chunk, 0, unroll=2)
        for group, targets in enumerate(Y_TARGETS):
            up = pltpu.roll(mixed_ref[group * 3], 1, 0)
            down = pltpu.roll(mixed_ref[group * 3 + 2], side - 1, 0)
            total = up + down
            results = (total + mixed_ref[group * 3 + 1], up - down, total)
            for my, target in enumerate(targets):
                moments_ref[target, z] = results[my]
                if 1 <= target <= 3:
                    speed_ref[target - 1, z, 0:side, :] = results[my]
                    speed_ref[target - 1, z, side : side + BXY, :] = results[my][0:BXY, :]

    def inner_rising(z):
        return lambda at: [post_ref[n, z - 1, at, :] for n in range(6)]

    def inner_falling(z):
        return lambda at: [post_ref[n, z + 1, at, :] for n in (6, 7, 8, 3, 4, 5)]

    def place(s, carry):
        first, column = place_ref[s, 0], place_ref[s, 2]
        window = ((lane - column) & (lanes - 1)) < BXY
        at = pl.multiple_of(s * BXY, BXY)
        for c in range(3):
            tile = boxes_ref[pl.ds(s * 3 + c, BXY, stride=rows), :]
            for z in range(planes):
                k = z - first
                turn = (column - BXY * k) & (lanes - 1)
                inside = window & (k >= 0) & (k < BZ)
                high, low = halves(jnp.where(inside, pltpu.roll(tile, turn, 1), 0.0))
                columns = pl.ds((c * planes + z) * lanes, lanes)
                rows_ref[pl.ds(at, BXY), columns] = high
                rows_ref[pl.ds(slots * BXY + at, BXY), columns] = low
        return carry

    def sample(s, carry):
        first, row, column = place_ref[s, 0], place_ref[s, 1], place_ref[s, 2]
        for c in range(3):
            tile = jnp.zeros((BXY, lanes), jnp.float32)
            for z in range(planes):
                k = z - first
                turn = (BXY * k - column) & (lanes - 1)
                moved = pltpu.roll(speed_ref[c, z, pl.ds(row, BXY), :], turn, 1)
                tile = jnp.where(unit == k, moved, tile)
            boxes_ref[pl.ds(s * 3 + c, BXY, stride=rows), :] = tile
        return carry

    def advance(first_step):
        coefs = -stiffness_ref[...] * held_ref[...]
        surface = dot_split(coefs, synth_high[...], synth_low[...], NT)
        boxes = dot_split(surface, spread_high[...], spread_low[...], NN)
        for i in range(BXY):
            boxes_ref[i * rows : (i + 1) * rows, :] = boxes[:, i * lanes : (i + 1) * lanes]
        lax.fori_loop(0, slots, place, 0)
        for c in range(3):
            for z in range(0, planes, 2):
                at = (c * planes + z) * lanes
                pair = dot(spots_ref[...], rows_ref[:, at : at + 2 * lanes], NN)
                force_ref[c, z] = pair[:, :lanes]
                force_ref[c, z + 1] = pair[:, lanes:]
        if first_step:
            load.wait()
        collide_plane(0)
        collide_plane(planes - 1)
        rise = remote(post_ref.at[pl.ds(0, 6), planes - 1], under_ref, 0, after)
        fall = remote(post_ref.at[pl.ds(3, 6), 0], over_ref, 1, before)
        rise.start()
        fall.start()

        def inner_collide(z, carry):
            collide_plane(z)
            return carry

        lax.fori_loop(1, planes - 1, inner_collide, 0)

        def inner_stream(z, carry):
            stream_plane(z, inner_rising(z), inner_falling(z))
            return carry

        lax.fori_loop(1, planes - 1, inner_stream, 0)
        rise.wait()
        stream_plane(0, lambda at: [under_ref[n, at, :] for n in range(6)], inner_falling(0))
        fall.wait()
        stream_plane(
            planes - 1, inner_rising(planes - 1),
            lambda at: [over_ref[n, at, :] for n in (3, 4, 5, 0, 1, 2)],
        )

    def project():
        lax.fori_loop(0, slots, sample, 0)
        sampled = jnp.concatenate(
            [boxes_ref[i * rows : (i + 1) * rows, :] for i in range(BXY)], axis=1
        )
        surface = dot_split(sampled, spread_high[...], spread_low[...], NT)
        return MOBILITY * dot_split(surface, synth_high[...], synth_low[...], NN)

    def swap():
        partial_ref[...] = project()
        onward = remote(partial_ref.at[pl.ds(block, shared)], below_ref, 2, after)
        back = remote(partial_ref.at[pl.ds(0, shared)], above_ref, 3, before)
        onward.start()
        back.start()
        held_ref[...] += partial_ref[...]
        onward.wait()
        held_ref[0:shared, :] += below_ref[...]
        back.wait()
        held_ref[block:, :] += above_ref[...]

    advance(True)
    swap()

    def step(iteration, carry):
        advance(False)
        swap()
        return carry

    lax.fori_loop(0, STEPS - 2, step, 0)
    advance(False)
    store = pltpu.make_async_copy(moments_ref, moments_out, local_sem.at[1])
    store.start()
    partial_ref[...] = project() + jnp.where(home_ref[...] > 0, held_ref[...], 0.0)
    copies = [
        remote(partial_ref.at[pl.ds(group * block, block)], final_ref.at[slot], 4 + slot, device)
        for slot, (group, device) in enumerate(((3, after), (1, before), (0, second_before)))
    ]
    for copy in copies:
        copy.start()
    for copy in copies:
        copy.wait()
    shapes_out[...] = (partial_ref[2 * block : 3 * block, :] + final_ref[0]) + (
        final_ref[1] + final_ref[2]
    )
    store.wait()


def per_device(moments, shapes, anchors, synthesis, spreading):
    planes, side, lanes = moments.shape[1:]
    devices = lax.axis_size("gz")
    total_planes = planes * devices
    first_plane = lax.axis_index("gz") * planes
    owned, parts, count = shapes.shape
    points = synthesis.shape[0]
    wide = -(-(count + 1) // 128) * 128
    block = owned * parts
    slots = GROUPS * owned
    rows = slots * parts
    shared = rows - block
    vmem = pl.BlockSpec(memory_space=pltpu.VMEM)
    smem = pl.BlockSpec(memory_space=pltpu.SMEM)
    anywhere = pl.BlockSpec(memory_space=pl.ANY)
    single = jnp.float32

    def struct(*shape, dtype=jnp.float32):
        return jax.ShapeDtypeStruct(shape, dtype)

    stiffness = jnp.pad(degree_stiffness(count), (0, wide - count))[None]
    packed = jnp.concatenate([shapes, anchors.astype(jnp.float32)[:, :, None]], axis=2)
    packed = jnp.pad(packed.reshape(block, count + 1), ((0, 0), (0, wide - count - 1)))
    held = jnp.concatenate(
        [shifted(packed, 2), shifted(packed, 1), packed, shifted(packed, -1)], axis=0
    )
    place = held[:, count].astype(jnp.int32).reshape(slots, 3)
    held = jnp.where(jnp.arange(wide) < count, held, 0.0)
    ahead = jnp.mod(place[:, 0] - first_plane, total_planes)
    ahead = jnp.where(ahead > total_planes - BZ, ahead - total_planes, ahead)
    home = ((ahead >= 0) & (ahead < planes)).astype(jnp.int32)
    home = jnp.broadcast_to(home[:, None, None], (slots, parts, wide)).reshape(rows, wide)
    place = jnp.stack([ahead, place[:, 1], place[:, 2]], axis=1)

    synth = jnp.pad(synthesis, ((0, 0), (0, wide - count)))
    synth_high = lax.reduce_precision(synth, 8, 7)
    synth_low = (synth - synth_high).astype(jnp.bfloat16)
    synth_high = synth_high.astype(jnp.bfloat16)
    spread_high, spread_low = pl.pallas_call(
        prepare_kernel,
        out_shape=[struct(points, spreading.shape[1], dtype=jnp.bfloat16)] * 2,
        in_specs=[vmem],
        out_specs=[vmem, vmem],
        compiler_params=pltpu.CompilerParams(vmem_limit_bytes=VMEM_LIMIT),
        cost_estimate=pl.CostEstimate(flops=50_000_000, bytes_accessed=8 << 20, transcendentals=0),
        name="prepare",
    )(spreading)

    def body(*refs):
        flow_kernel(devices, *refs)

    moments, result = pl.pallas_call(
        body,
        out_shape=[struct(10, planes, side, lanes), struct(block, wide)],
        in_specs=[smem, anywhere] + [vmem] * 7,
        out_specs=[anywhere, vmem],
        scratch_shapes=[
            pltpu.VMEM((10, planes, side, lanes), single),
            pltpu.VMEM((10, planes, side, lanes), single),
            pltpu.VMEM((3, planes, side, lanes), single),
            pltpu.VMEM((3, planes, side + BXY, lanes), single),
            pltpu.VMEM((18, side, lanes), single),
            pltpu.VMEM((BXY * rows, lanes), single),
            pltpu.VMEM((side, 2 * slots * BXY), jnp.bfloat16),
            pltpu.VMEM((2 * slots * BXY, 3 * planes * lanes), jnp.bfloat16),
            pltpu.VMEM((rows, wide), single),
            pltpu.VMEM((rows, wide), single),
            pltpu.VMEM((shared, wide), single),
            pltpu.VMEM((shared, wide), single),
            pltpu.VMEM((6, side, lanes), single),
            pltpu.VMEM((6, side, lanes), single),
            pltpu.VMEM((3, block, wide), single),
            pltpu.SemaphoreType.DMA((2,)),
            pltpu.SemaphoreType.DMA((7,)),
            pltpu.SemaphoreType.DMA((7,)),
        ],
        compiler_params=pltpu.CompilerParams(
            vmem_limit_bytes=VMEM_LIMIT, collective_id=0, has_side_effects=True
        ),
        name="flow",
    )(place, moments, held, home, stiffness, synth_high, synth_low, spread_high, spread_low)
    return moments, result[:, :count].reshape(owned, parts, count)


def solution(mesh):
    return jax.shard_map(
        per_device,
        mesh=mesh,
        in_specs=(P(None, "gz", None, None), P("gz", None, None), P("gz", None), P(), P()),
        out_specs=(P(None, "gz", None, None), P("gz", None, None)),
        check_vma=False,
    )
```

```python
import jax
import jax.numpy as jnp
from jax import lax
from jax.experimental import pallas as pl
from jax.experimental.pallas import tpu as pltpu
from jax.sharding import PartitionSpec as P

LMAX = 16
BZ = 8
BXY = 16
STEPS = 3

RELAX_RATE = 1.25
STIFF_SCALE = 0.002
MOBILITY = 0.5
GROUPS = 4
ROWS = 16
NN = (((1,), (0,)), ((), ()))
NT = (((1,), (1,)), ((), ()))
VMEM_LIMIT = 36 * 1024 * 1024


def shifted(block, distance):
    count = lax.axis_size("gz")
    return lax.ppermute(block, "gz", [((i - distance) % count, i) for i in range(count)])


def degree_stiffness(coefficient_count):
    numbers = jnp.arange(coefficient_count, dtype=jnp.int32)
    degree = jnp.zeros((coefficient_count,), jnp.int32)
    for degree_step in range(1, LMAX + 1):
        degree = degree + (numbers >= degree_step * degree_step).astype(jnp.int32)
    return STIFF_SCALE * (degree * (degree + 1) + 2).astype(jnp.float32)


def halves(value):
    high = value.astype(jnp.bfloat16)
    low = (value - high.astype(jnp.float32)).astype(jnp.bfloat16)
    return high, low


def dot(a, b, dims):
    return lax.dot_general(a, b, dims, preferred_element_type=jnp.float32)


def dot_split(value, high, low, dims):
    value_high, value_low = halves(value)
    return dot(value_high, high, dims) + (dot(value_low, high, dims) + dot(value_high, low, dims))


def prepare_kernel(spreading_ref, high_ref, low_ref):
    lanes = BZ * BXY
    row_count = spreading_ref.shape[0]
    unit = lax.broadcasted_iota(jnp.int32, (16, lanes), 1) // BXY

    def chunk(index, carry):
        rows = pl.ds(pl.multiple_of(index * 16, 16), 16)
        for half in range(BXY // BZ):
            tiles = [
                spreading_ref[rows, pl.ds((k * (BXY // BZ) + half) * lanes, lanes)]
                for k in range(BZ)
            ]
            distance = 1
            while distance < BZ:
                upper = (unit & distance) != 0
                for a in range(BZ):
                    if a & distance == 0:
                        b = a + distance
                        left = jnp.where(upper, pltpu.roll(tiles[b], distance * BXY, 1), tiles[a])
                        right = jnp.where(
                            upper, tiles[b], pltpu.roll(tiles[a], lanes - distance * BXY, 1)
                        )
                        tiles[a], tiles[b] = left, right
                distance *= 2
            for position in range(BZ):
                high, low = halves(tiles[position])
                columns = pl.ds((half * BZ + position) * lanes, lanes)
                high_ref[rows, columns] = high
                low_ref[rows, columns] = low
        return carry

    lax.fori_loop(0, row_count // 16, chunk, 0, unroll=4)


def hermite_split(a0, a1, a2):
    base = a0 * (1.0 / 6.0)
    if a2 is not None:
        base = base + 0.5 * a2
    rest = a0 * (2.0 / 3.0)
    if a2 is not None:
        rest = rest - a2
    if a1 is None:
        return base, rest, base
    odd = 0.5 * a1
    return base + odd, rest, base - odd


Y_GROUPS = ((0, 0), (1, 0), (0, 1), (2, 0), (0, 2), (1, 1))
Y_TARGETS = ((0, 2, 5), (1, 7), (3, 9), (4,), (6,), (8,))


def collide_cell(moments, force):
    rho, jz, jy, jx, zz, yy, xx, zy, zx, yx = moments
    fz, fy, fx = force
    uz, uy, ux = jz + 0.5 * fz, jy + 0.5 * fy, jx + 0.5 * fx
    third = rho * (1.0 / 3.0)
    half_source = 1.0 - 0.5 * RELAX_RATE

    def second(current, target, source):
        return current + RELAX_RATE * (target - current) + half_source * source

    zz = second(zz, uz * uz + third, 2.0 * (fz * uz))
    yy = second(yy, uy * uy + third, 2.0 * (fy * uy))
    xx = second(xx, ux * ux + third, 2.0 * (fx * ux))
    zy = second(zy, uz * uy, fz * uy + uz * fy)
    zx = second(zx, uz * ux, fz * ux + uz * fx)
    yx = second(yx, uy * ux, fy * ux + uy * fx)
    jz, jy, jx = 0.5 * (jz + fz), (jy + fy) * (1.0 / 6.0), (jx + fx) * (1.0 / 6.0)
    zz_half, zy, zx = 0.5 * zz, 0.5 * zy, 0.5 * zx
    return (
        zz_half + jz, jy + zy, jx + zx,
        (yy - third) * (1.0 / 6.0), (xx - third) * (1.0 / 6.0), yx * (1.0 / 6.0),
        zz_half - jz, jy - zy, jx - zx,
        rho - zz,
    )


def mix_cell(rising, here, falling, lanes):
    rest = [
        here[9], 2.0 * (here[1] + here[7]), 2.0 * (here[2] + here[8]),
        4.0 * here[3], 4.0 * here[4], 4.0 * here[5],
    ]
    along_z = []
    for g in range(6):
        total = rising[g] + falling[g]
        along_z.append((total + rest[g], rising[g] - falling[g], total))
    mixed = [None] * 18
    for mz in range(3):
        one, in_y, in_x, in_yy, in_xx, in_yx = [along_z[g][mz] for g in range(6)]
        along_x = []
        for a0, a1, a2 in ((one, in_x, in_xx), (in_y, in_yx, None), (in_yy, None, None)):
            right, stay, left = hermite_split(a0, a1, a2)
            right = pltpu.roll(right, 1, 1)
            left = pltpu.roll(left, lanes - 1, 1)
            total = right + left
            along_x.append((total + stay, right - left, total))
        for mx in range(3 - mz):
            group = Y_GROUPS.index((mz, mx))
            parts = hermite_split(along_x[0][mx], along_x[1][mx], along_x[2][mx])
            for n in range(3):
                mixed[group * 3 + n] = parts[n]
    return mixed


def flow_kernel(
    devices, place_ref, moments_in, shapes_ref, home_ref, stiffness_ref,
    synth_high, synth_low, spread_high, spread_low,
    moments_out, shapes_out,
    moments_ref, post_ref, force_ref, speed_ref, mixed_ref, boxes_ref, spots_ref, rows_ref, held_ref,
    partial_ref, below_ref, above_ref, under_ref, over_ref, final_ref,
    local_sem, send_sem, recv_sem,
):
    planes, side, lanes = moments_ref.shape[1:]
    rows = shapes_ref.shape[0]
    slots = rows // 3
    block = rows // GROUPS
    shared = rows - block
    chunks = side // ROWS
    me = lax.axis_index("gz")
    after, before = lax.rem(me + 1, devices), lax.rem(me + devices - 1, devices)
    second_after, second_before = lax.rem(me + 2, devices), lax.rem(me + devices - 2, devices)

    load = pltpu.make_async_copy(moments_in, moments_ref, local_sem.at[0])
    load.start()
    barrier = pltpu.get_barrier_semaphore()
    for other in (before, after, second_before, second_after):
        pl.semaphore_signal(
            barrier, inc=1, device_id=(other,), device_id_type=pl.DeviceIdType.MESH
        )
    pl.semaphore_wait(barrier, 4)

    def remote(source, target, number, device):
        return pltpu.make_async_remote_copy(
            src_ref=source, dst_ref=target, send_sem=send_sem.at[number],
            recv_sem=recv_sem.at[number], device_id=(device,),
            device_id_type=pl.DeviceIdType.MESH,
        )

    lane = lax.broadcasted_iota(jnp.int32, (BXY, lanes), 1)
    depth = lax.broadcasted_iota(jnp.int32, (BXY, lanes), 0)
    unit = lane // BXY

    def spot(s, carry):
        hit = ((lane - place_ref[s, 1] - depth) & (side - 1)) == 0
        boxes_ref[pl.ds(pl.multiple_of(s * BXY, BXY), BXY), :] = jnp.where(hit, 1.0, 0.0)
        return carry

    lax.fori_loop(0, slots, spot, 0, unroll=4)
    spots = boxes_ref[0 : slots * BXY, :].T.astype(jnp.bfloat16)
    spots_ref[:, 0 : slots * BXY] = spots
    spots_ref[:, slots * BXY :] = spots
    held_ref[...] = shapes_ref[...]

    def collide_plane(z):
        def chunk(index, carry):
            at = pl.ds(pl.multiple_of(index * ROWS, ROWS), ROWS)
            fields = collide_cell(
                [moments_ref[n, z, at, :] for n in range(10)],
                [force_ref[c, z, at, :] for c in range(3)],
            )
            for n in range(10):
                post_ref[n, z, at, :] = fields[n]
            return carry

        lax.fori_loop(0, chunks, chunk, 0, unroll=2)

    def stream_plane(z, rising, falling):
        def chunk(index, carry):
            at = pl.ds(pl.multiple_of(index * ROWS, ROWS), ROWS)
            here = [post_ref[n, z, at, :] for n in range(10)]
            mixed = mix_cell(rising(at), here, falling(at), lanes)
            for n in range(18):
                mixed_ref[n, at, :] = mixed[n]
            return carry

        lax.fori_loop(0, chunks, chunk, 0, unroll=2)
        for group, targets in enumerate(Y_TARGETS):
            up = pltpu.roll(mixed_ref[group * 3], 1, 0)
            down = pltpu.roll(mixed_ref[group * 3 + 2], side - 1, 0)
            total = up + down
            results = (total + mixed_ref[group * 3 + 1], up - down, total)
            for my, target in enumerate(targets):
                moments_ref[target, z] = results[my]
                if 1 <= target <= 3:
                    speed_ref[target - 1, z, 0:side, :] = results[my]
                    speed_ref[target - 1, z, side : side + BXY, :] = results[my][0:BXY, :]

    def inner_rising(z):
        return lambda at: [post_ref[n, z - 1, at, :] for n in range(6)]

    def inner_falling(z):
        return lambda at: [post_ref[n, z + 1, at, :] for n in (6, 7, 8, 3, 4, 5)]

    def place(s, carry):
        first, column = place_ref[s, 0], place_ref[s, 2]
        window = ((lane - column) & (lanes - 1)) < BXY
        at = pl.multiple_of(s * BXY, BXY)
        for c in range(3):
            tile = boxes_ref[pl.ds(s * 3 + c, BXY, stride=rows), :]
            for z in range(planes):
                k = z - first
                turn = (column - BXY * k) & (lanes - 1)
                inside = window & (k >= 0) & (k < BZ)
                high, low = halves(jnp.where(inside, pltpu.roll(tile, turn, 1), 0.0))
                columns = pl.ds((c * planes + z) * lanes, lanes)
                rows_ref[pl.ds(at, BXY), columns] = high
                rows_ref[pl.ds(slots * BXY + at, BXY), columns] = low
        return carry

    def sample(s, carry):
        first, row, column = place_ref[s, 0], place_ref[s, 1], place_ref[s, 2]
        for c in range(3):
            tile = jnp.zeros((BXY, lanes), jnp.float32)
            for z in range(planes):
                k = z - first
                turn = (BXY * k - column) & (lanes - 1)
                moved = pltpu.roll(speed_ref[c, z, pl.ds(row, BXY), :], turn, 1)
                tile = jnp.where(unit == k, moved, tile)
            boxes_ref[pl.ds(s * 3 + c, BXY, stride=rows), :] = tile
        return carry

    def advance(first_step):
        coefs = -stiffness_ref[...] * held_ref[...]
        surface = dot_split(coefs, synth_high[...], synth_low[...], NT)
        boxes = dot_split(surface, spread_high[...], spread_low[...], NN)
        for i in range(BXY):
            boxes_ref[i * rows : (i + 1) * rows, :] = boxes[:, i * lanes : (i + 1) * lanes]
        lax.fori_loop(0, slots, place, 0, unroll=4)
        for c in range(3):
            for z in range(0, planes, 2):
                at = (c * planes + z) * lanes
                pair = dot(spots_ref[...], rows_ref[:, at : at + 2 * lanes], NN)
                force_ref[c, z] = pair[:, :lanes]
                force_ref[c, z + 1] = pair[:, lanes:]
        if first_step:
            load.wait()
        collide_plane(0)
        collide_plane(planes - 1)
        rise = remote(post_ref.at[pl.ds(0, 6), planes - 1], under_ref, 0, after)
        fall = remote(post_ref.at[pl.ds(3, 6), 0], over_ref, 1, before)
        rise.start()
        fall.start()

        def inner_collide(z, carry):
            collide_plane(z)
            return carry

        lax.fori_loop(1, planes - 1, inner_collide, 0)

        def inner_stream(z, carry):
            stream_plane(z, inner_rising(z), inner_falling(z))
            return carry

        lax.fori_loop(1, planes - 1, inner_stream, 0)
        rise.wait()
        stream_plane(0, lambda at: [under_ref[n, at, :] for n in range(6)], inner_falling(0))
        fall.wait()
        stream_plane(
            planes - 1, inner_rising(planes - 1),
            lambda at: [over_ref[n, at, :] for n in (3, 4, 5, 0, 1, 2)],
        )

    def project():
        lax.fori_loop(0, slots, sample, 0, unroll=4)
        sampled = jnp.concatenate(
            [boxes_ref[i * rows : (i + 1) * rows, :] for i in range(BXY)], axis=1
        )
        sampled_high, sampled_low = halves(sampled)
        both = jnp.concatenate([sampled_high, sampled_low], axis=0)
        surface = dot(spread_high[...], both, NT)
        surface = surface[:, :rows] + (
            surface[:, rows:] + dot(spread_low[...], sampled_high, NT)
        )
        return MOBILITY * dot_split(surface.T, synth_high[...], synth_low[...], NN)

    def swap():
        partial_ref[...] = project()
        onward = remote(partial_ref.at[pl.ds(block, shared)], below_ref, 2, after)
        back = remote(partial_ref.at[pl.ds(0, shared)], above_ref, 3, before)
        onward.start()
        back.start()
        held_ref[...] += partial_ref[...]
        onward.wait()
        held_ref[0:shared, :] += below_ref[...]
        back.wait()
        held_ref[block:, :] += above_ref[...]

    advance(True)
    swap()

    def step(iteration, carry):
        advance(False)
        swap()
        return carry

    lax.fori_loop(0, STEPS - 2, step, 0)
    advance(False)
    store = pltpu.make_async_copy(moments_ref, moments_out, local_sem.at[1])
    store.start()
    partial_ref[...] = project() + jnp.where(home_ref[...] > 0, held_ref[...], 0.0)
    copies = [
        remote(partial_ref.at[pl.ds(group * block, block)], final_ref.at[slot], 4 + slot, device)
        for slot, (group, device) in enumerate(((3, after), (1, before), (0, second_before)))
    ]
    for copy in copies:
        copy.start()
    for copy in copies:
        copy.wait()
    shapes_out[...] = (partial_ref[2 * block : 3 * block, :] + final_ref[0]) + (
        final_ref[1] + final_ref[2]
    )
    store.wait()


def per_device(moments, shapes, anchors, synthesis, spreading):
    planes, side, lanes = moments.shape[1:]
    devices = lax.axis_size("gz")
    total_planes = planes * devices
    first_plane = lax.axis_index("gz") * planes
    owned, parts, count = shapes.shape
    points = synthesis.shape[0]
    wide = -(-(count + 1) // 128) * 128
    block = owned * parts
    slots = GROUPS * owned
    rows = slots * parts
    shared = rows - block
    vmem = pl.BlockSpec(memory_space=pltpu.VMEM)
    smem = pl.BlockSpec(memory_space=pltpu.SMEM)
    anywhere = pl.BlockSpec(memory_space=pl.ANY)
    single = jnp.float32

    def struct(*shape, dtype=jnp.float32):
        return jax.ShapeDtypeStruct(shape, dtype)

    stiffness = jnp.pad(degree_stiffness(count), (0, wide - count))[None]
    packed = jnp.concatenate([shapes, anchors.astype(jnp.float32)[:, :, None]], axis=2)
    packed = jnp.pad(packed.reshape(block, count + 1), ((0, 0), (0, wide - count - 1)))
    held = jnp.concatenate(
        [shifted(packed, 2), shifted(packed, 1), packed, shifted(packed, -1)], axis=0
    )
    place = held[:, count].astype(jnp.int32).reshape(slots, 3)
    held = jnp.where(jnp.arange(wide) < count, held, 0.0)
    ahead = jnp.mod(place[:, 0] - first_plane, total_planes)
    ahead = jnp.where(ahead > total_planes - BZ, ahead - total_planes, ahead)
    home = ((ahead >= 0) & (ahead < planes)).astype(jnp.int32)
    home = jnp.broadcast_to(home[:, None, None], (slots, parts, wide)).reshape(rows, wide)
    place = jnp.stack([ahead, place[:, 1], place[:, 2]], axis=1)

    synth = jnp.pad(synthesis, ((0, 0), (0, wide - count)))
    synth_high = lax.reduce_precision(synth, 8, 7)
    synth_low = (synth - synth_high).astype(jnp.bfloat16)
    synth_high = synth_high.astype(jnp.bfloat16)
    spread_high, spread_low = pl.pallas_call(
        prepare_kernel,
        out_shape=[struct(points, spreading.shape[1], dtype=jnp.bfloat16)] * 2,
        in_specs=[vmem],
        out_specs=[vmem, vmem],
        compiler_params=pltpu.CompilerParams(vmem_limit_bytes=VMEM_LIMIT),
        cost_estimate=pl.CostEstimate(flops=50_000_000, bytes_accessed=8 << 20, transcendentals=0),
        name="prepare",
    )(spreading)

    def body(*refs):
        flow_kernel(devices, *refs)

    moments, result = pl.pallas_call(
        body,
        out_shape=[struct(10, planes, side, lanes), struct(block, wide)],
        in_specs=[smem, anywhere] + [vmem] * 7,
        out_specs=[anywhere, vmem],
        scratch_shapes=[
            pltpu.VMEM((10, planes, side, lanes), single),
            pltpu.VMEM((10, planes, side, lanes), single),
            pltpu.VMEM((3, planes, side, lanes), single),
            pltpu.VMEM((3, planes, side + BXY, lanes), single),
            pltpu.VMEM((18, side, lanes), single),
            pltpu.VMEM((BXY * rows, lanes), single),
            pltpu.VMEM((side, 2 * slots * BXY), jnp.bfloat16),
            pltpu.VMEM((2 * slots * BXY, 3 * planes * lanes), jnp.bfloat16),
            pltpu.VMEM((rows, wide), single),
            pltpu.VMEM((rows, wide), single),
            pltpu.VMEM((shared, wide), single),
            pltpu.VMEM((shared, wide), single),
            pltpu.VMEM((6, side, lanes), single),
            pltpu.VMEM((6, side, lanes), single),
            pltpu.VMEM((3, block, wide), single),
            pltpu.SemaphoreType.DMA((2,)),
            pltpu.SemaphoreType.DMA((7,)),
            pltpu.SemaphoreType.DMA((7,)),
        ],
        compiler_params=pltpu.CompilerParams(
            vmem_limit_bytes=VMEM_LIMIT, collective_id=0, has_side_effects=True
        ),
        name="flow",
    )(place, moments, held, home, stiffness, synth_high, synth_low, spread_high, spread_low)
    return moments, result[:, :count].reshape(owned, parts, count)


def solution(mesh):
    return jax.shard_map(
        per_device,
        mesh=mesh,
        in_specs=(P(None, "gz", None, None), P("gz", None, None), P("gz", None), P(), P()),
        out_specs=(P(None, "gz", None, None), P("gz", None, None)),
        check_vma=False,
    )
```

```python
import jax
import jax.numpy as jnp
from jax import lax
from jax.experimental import pallas as pl
from jax.experimental.pallas import tpu as pltpu
from jax.sharding import PartitionSpec as P

LMAX = 16
BZ = 8
BXY = 16
STEPS = 3

RELAX_RATE = 1.25
STIFF_SCALE = 0.002
MOBILITY = 0.5
GROUPS = 4
ROWS = 16
NN = (((1,), (0,)), ((), ()))
NT = (((1,), (1,)), ((), ()))
VMEM_LIMIT = 36 * 1024 * 1024


def shifted(block, distance):
    count = lax.axis_size("gz")
    return lax.ppermute(block, "gz", [((i - distance) % count, i) for i in range(count)])


def degree_stiffness(coefficient_count):
    numbers = jnp.arange(coefficient_count, dtype=jnp.int32)
    degree = jnp.zeros((coefficient_count,), jnp.int32)
    for degree_step in range(1, LMAX + 1):
        degree = degree + (numbers >= degree_step * degree_step).astype(jnp.int32)
    return STIFF_SCALE * (degree * (degree + 1) + 2).astype(jnp.float32)


def halves(value):
    high = value.astype(jnp.bfloat16)
    low = (value - high.astype(jnp.float32)).astype(jnp.bfloat16)
    return high, low


def dot(a, b, dims):
    return lax.dot_general(a, b, dims, preferred_element_type=jnp.float32)


def dot_split(value, high, low, dims):
    value_high, value_low = halves(value)
    return dot(value_high, high, dims) + (dot(value_low, high, dims) + dot(value_high, low, dims))


def prepare_kernel(spreading_ref, synthesis_ref, high_ref, low_ref, synth_high, synth_low):
    count = synthesis_ref.shape[1]
    synth_high[...] = jnp.zeros_like(synth_high)
    synth_low[...] = jnp.zeros_like(synth_low)
    synth_high[:, 0:count], synth_low[:, 0:count] = halves(synthesis_ref[...])
    lanes = BZ * BXY
    row_count = spreading_ref.shape[0]
    unit = lax.broadcasted_iota(jnp.int32, (16, lanes), 1) // BXY

    def chunk(index, carry):
        rows = pl.ds(pl.multiple_of(index * 16, 16), 16)
        for half in range(BXY // BZ):
            tiles = [
                spreading_ref[rows, pl.ds((k * (BXY // BZ) + half) * lanes, lanes)]
                for k in range(BZ)
            ]
            distance = 1
            while distance < BZ:
                upper = (unit & distance) != 0
                for a in range(BZ):
                    if a & distance == 0:
                        b = a + distance
                        left = jnp.where(upper, pltpu.roll(tiles[b], distance * BXY, 1), tiles[a])
                        right = jnp.where(
                            upper, tiles[b], pltpu.roll(tiles[a], lanes - distance * BXY, 1)
                        )
                        tiles[a], tiles[b] = left, right
                distance *= 2
            for position in range(BZ):
                high, low = halves(tiles[position])
                columns = pl.ds((half * BZ + position) * lanes, lanes)
                high_ref[rows, columns] = high
                low_ref[rows, columns] = low
        return carry

    lax.fori_loop(0, row_count // 16, chunk, 0, unroll=4)


def hermite_split(a0, a1, a2):
    base = a0 * (1.0 / 6.0)
    if a2 is not None:
        base = base + 0.5 * a2
    rest = a0 * (2.0 / 3.0)
    if a2 is not None:
        rest = rest - a2
    if a1 is None:
        return base, rest, base
    odd = 0.5 * a1
    return base + odd, rest, base - odd


Y_GROUPS = ((0, 0), (1, 0), (0, 1), (2, 0), (0, 2), (1, 1))
Y_TARGETS = ((0, 2, 5), (1, 7), (3, 9), (4,), (6,), (8,))


def collide_cell(moments, force):
    rho, jz, jy, jx, zz, yy, xx, zy, zx, yx = moments
    fz, fy, fx = force
    uz, uy, ux = jz + 0.5 * fz, jy + 0.5 * fy, jx + 0.5 * fx
    third = rho * (1.0 / 3.0)
    half_source = 1.0 - 0.5 * RELAX_RATE

    def second(current, target, source):
        return current + RELAX_RATE * (target - current) + half_source * source

    zz = second(zz, uz * uz + third, 2.0 * (fz * uz))
    yy = second(yy, uy * uy + third, 2.0 * (fy * uy))
    xx = second(xx, ux * ux + third, 2.0 * (fx * ux))
    zy = second(zy, uz * uy, fz * uy + uz * fy)
    zx = second(zx, uz * ux, fz * ux + uz * fx)
    yx = second(yx, uy * ux, fy * ux + uy * fx)
    jz, jy, jx = 0.5 * (jz + fz), (jy + fy) * (1.0 / 6.0), (jx + fx) * (1.0 / 6.0)
    zz_half, zy, zx = 0.5 * zz, 0.5 * zy, 0.5 * zx
    return (
        zz_half + jz, jy + zy, jx + zx,
        (yy - third) * (1.0 / 6.0), (xx - third) * (1.0 / 6.0), yx * (1.0 / 6.0),
        zz_half - jz, jy - zy, jx - zx,
        rho - zz,
    )


def mix_cell(rising, here, falling, lanes):
    rest = [
        here[9], 2.0 * (here[1] + here[7]), 2.0 * (here[2] + here[8]),
        4.0 * here[3], 4.0 * here[4], 4.0 * here[5],
    ]
    along_z = []
    for g in range(6):
        total = rising[g] + falling[g]
        along_z.append((total + rest[g], rising[g] - falling[g], total))
    mixed = [None] * 18
    for mz in range(3):
        one, in_y, in_x, in_yy, in_xx, in_yx = [along_z[g][mz] for g in range(6)]
        along_x = []
        for a0, a1, a2 in ((one, in_x, in_xx), (in_y, in_yx, None), (in_yy, None, None)):
            right, stay, left = hermite_split(a0, a1, a2)
            right = pltpu.roll(right, 1, 1)
            left = pltpu.roll(left, lanes - 1, 1)
            total = right + left
            along_x.append((total + stay, right - left, total))
        for mx in range(3 - mz):
            group = Y_GROUPS.index((mz, mx))
            parts = hermite_split(along_x[0][mx], along_x[1][mx], along_x[2][mx])
            for n in range(3):
                mixed[group * 3 + n] = parts[n]
    return mixed


def flow_kernel(
    devices, place_ref, moments_in, shapes_ref, home_ref, stiffness_ref,
    synth_high, synth_low, spread_high, spread_low,
    moments_out, shapes_out,
    moments_ref, post_ref, force_ref, speed_ref, mixed_ref, boxes_ref, spots_ref, rows_ref, held_ref,
    partial_ref, below_ref, above_ref, under_ref, over_ref, final_ref,
    local_sem, send_sem, recv_sem,
):
    planes, side, lanes = moments_ref.shape[1:]
    rows = shapes_ref.shape[0]
    slots = rows // 3
    block = rows // GROUPS
    shared = rows - block
    chunks = side // ROWS
    me = lax.axis_index("gz")
    after, before = lax.rem(me + 1, devices), lax.rem(me + devices - 1, devices)
    second_after, second_before = lax.rem(me + 2, devices), lax.rem(me + devices - 2, devices)

    load = pltpu.make_async_copy(moments_in, moments_ref, local_sem.at[0])
    load.start()
    barrier = pltpu.get_barrier_semaphore()
    for other in (before, after, second_before, second_after):
        pl.semaphore_signal(
            barrier, inc=1, device_id=(other,), device_id_type=pl.DeviceIdType.MESH
        )
    pl.semaphore_wait(barrier, 4)

    def remote(source, target, number, device):
        return pltpu.make_async_remote_copy(
            src_ref=source, dst_ref=target, send_sem=send_sem.at[number],
            recv_sem=recv_sem.at[number], device_id=(device,),
            device_id_type=pl.DeviceIdType.MESH,
        )

    lane = lax.broadcasted_iota(jnp.int32, (BXY, lanes), 1)
    depth = lax.broadcasted_iota(jnp.int32, (BXY, lanes), 0)
    unit = lane // BXY

    def spot(s, carry):
        hit = ((lane - place_ref[s, 1] - depth) & (side - 1)) == 0
        boxes_ref[pl.ds(pl.multiple_of(s * BXY, BXY), BXY), :] = jnp.where(hit, 1.0, 0.0)
        return carry

    lax.fori_loop(0, slots, spot, 0, unroll=4)
    spots = boxes_ref[0 : slots * BXY, :].T.astype(jnp.bfloat16)
    spots_ref[:, 0 : slots * BXY] = spots
    spots_ref[:, slots * BXY :] = spots
    held_ref[...] = shapes_ref[...]

    def collide_plane(z):
        def chunk(index, carry):
            at = pl.ds(pl.multiple_of(index * ROWS, ROWS), ROWS)
            fields = collide_cell(
                [moments_ref[n, z, at, :] for n in range(10)],
                [force_ref[c, z, at, :] for c in range(3)],
            )
            for n in range(10):
                post_ref[n, z, at, :] = fields[n]
            return carry

        lax.fori_loop(0, chunks, chunk, 0, unroll=2)

    def stream_plane(z, rising, falling):
        def chunk(index, carry):
            at = pl.ds(pl.multiple_of(index * ROWS, ROWS), ROWS)
            here = [post_ref[n, z, at, :] for n in range(10)]
            mixed = mix_cell(rising(at), here, falling(at), lanes)
            for n in range(18):
                mixed_ref[n, at, :] = mixed[n]
            return carry

        lax.fori_loop(0, chunks, chunk, 0, unroll=2)
        for group, targets in enumerate(Y_TARGETS):
            up = pltpu.roll(mixed_ref[group * 3], 1, 0)
            down = pltpu.roll(mixed_ref[group * 3 + 2], side - 1, 0)
            total = up + down
            results = (total + mixed_ref[group * 3 + 1], up - down, total)
            for my, target in enumerate(targets):
                moments_ref[target, z] = results[my]
                if 1 <= target <= 3:
                    speed_ref[target - 1, z, 0:side, :] = results[my]
                    speed_ref[target - 1, z, side : side + BXY, :] = results[my][0:BXY, :]

    def inner_rising(z):
        return lambda at: [post_ref[n, z - 1, at, :] for n in range(6)]

    def inner_falling(z):
        return lambda at: [post_ref[n, z + 1, at, :] for n in (6, 7, 8, 3, 4, 5)]

    def place(s, carry):
        first, column = place_ref[s, 0], place_ref[s, 2]
        window = ((lane - column) & (lanes - 1)) < BXY
        at = pl.multiple_of(s * BXY, BXY)
        for c in range(3):
            tile = boxes_ref[pl.ds(s * 3 + c, BXY, stride=rows), :]
            for z in range(planes):
                k = z - first
                turn = (column - BXY * k) & (lanes - 1)
                inside = window & (k >= 0) & (k < BZ)
                high, low = halves(jnp.where(inside, pltpu.roll(tile, turn, 1), 0.0))
                columns = pl.ds((c * planes + z) * lanes, lanes)
                rows_ref[pl.ds(at, BXY), columns] = high
                rows_ref[pl.ds(slots * BXY + at, BXY), columns] = low
        return carry

    def sample(s, carry):
        first, row, column = place_ref[s, 0], place_ref[s, 1], place_ref[s, 2]
        for c in range(3):
            tile = jnp.zeros((BXY, lanes), jnp.float32)
            for z in range(planes):
                k = z - first
                turn = (BXY * k - column) & (lanes - 1)
                moved = pltpu.roll(speed_ref[c, z, pl.ds(row, BXY), :], turn, 1)
                tile = jnp.where(unit == k, moved, tile)
            boxes_ref[pl.ds(s * 3 + c, BXY, stride=rows), :] = tile
        return carry

    def advance(first_step):
        coefs = -stiffness_ref[...] * held_ref[...]
        surface = dot_split(coefs, synth_high[...], synth_low[...], NT)
        boxes = dot_split(surface, spread_high[...], spread_low[...], NN)
        for i in range(BXY):
            boxes_ref[i * rows : (i + 1) * rows, :] = boxes[:, i * lanes : (i + 1) * lanes]
        lax.fori_loop(0, slots, place, 0, unroll=4)
        for c in range(3):
            for z in range(0, planes, 2):
                at = (c * planes + z) * lanes
                pair = dot(spots_ref[...], rows_ref[:, at : at + 2 * lanes], NN)
                force_ref[c, z] = pair[:, :lanes]
                force_ref[c, z + 1] = pair[:, lanes:]
        if first_step:
            load.wait()
        collide_plane(0)
        collide_plane(planes - 1)
        rise = remote(post_ref.at[pl.ds(0, 6), planes - 1], under_ref, 0, after)
        fall = remote(post_ref.at[pl.ds(3, 6), 0], over_ref, 1, before)
        rise.start()
        fall.start()

        def inner_collide(z, carry):
            collide_plane(z)
            return carry

        lax.fori_loop(1, planes - 1, inner_collide, 0)

        def inner_stream(z, carry):
            stream_plane(z, inner_rising(z), inner_falling(z))
            return carry

        lax.fori_loop(1, planes - 1, inner_stream, 0)
        rise.wait()
        stream_plane(0, lambda at: [under_ref[n, at, :] for n in range(6)], inner_falling(0))
        fall.wait()
        stream_plane(
            planes - 1, inner_rising(planes - 1),
            lambda at: [over_ref[n, at, :] for n in (3, 4, 5, 0, 1, 2)],
        )

    def project():
        lax.fori_loop(0, slots, sample, 0, unroll=4)
        sampled = jnp.concatenate(
            [boxes_ref[i * rows : (i + 1) * rows, :] for i in range(BXY)], axis=1
        )
        sampled_high, sampled_low = halves(sampled)
        both = jnp.concatenate([sampled_high, sampled_low], axis=0)
        surface = dot(spread_high[...], both, NT)
        surface = surface[:, :rows] + (
            surface[:, rows:] + dot(spread_low[...], sampled_high, NT)
        )
        return MOBILITY * dot_split(surface.T, synth_high[...], synth_low[...], NN)

    def swap():
        partial_ref[...] = project()
        onward = remote(partial_ref.at[pl.ds(block, shared)], below_ref, 2, after)
        back = remote(partial_ref.at[pl.ds(0, shared)], above_ref, 3, before)
        onward.start()
        back.start()
        held_ref[...] += partial_ref[...]
        onward.wait()
        held_ref[0:shared, :] += below_ref[...]
        back.wait()
        held_ref[block:, :] += above_ref[...]

    advance(True)
    swap()

    def step(iteration, carry):
        advance(False)
        swap()
        return carry

    lax.fori_loop(0, STEPS - 2, step, 0)
    advance(False)
    store = pltpu.make_async_copy(moments_ref, moments_out, local_sem.at[1])
    store.start()
    partial_ref[...] = project() + jnp.where(home_ref[...] > 0, held_ref[...], 0.0)
    copies = [
        remote(partial_ref.at[pl.ds(group * block, block)], final_ref.at[slot], 4 + slot, device)
        for slot, (group, device) in enumerate(((3, after), (1, before), (0, second_before)))
    ]
    for copy in copies:
        copy.start()
    for copy in copies:
        copy.wait()
    shapes_out[...] = (partial_ref[2 * block : 3 * block, :] + final_ref[0]) + (
        final_ref[1] + final_ref[2]
    )
    store.wait()


def store_kernel(source_ref, target_ref, sem):
    copies = [
        pltpu.make_async_copy(source_ref.at[n], target_ref.at[n], sem.at[n]) for n in range(10)
    ]
    for copy in copies:
        copy.start()
    for copy in copies:
        copy.wait()


def per_device(moments, shapes, anchors, synthesis, spreading):
    planes, side, lanes = moments.shape[1:]
    devices = lax.axis_size("gz")
    total_planes = planes * devices
    first_plane = lax.axis_index("gz") * planes
    owned, parts, count = shapes.shape
    points = synthesis.shape[0]
    wide = -(-(count + 1) // 128) * 128
    block = owned * parts
    slots = GROUPS * owned
    rows = slots * parts
    shared = rows - block
    vmem = pl.BlockSpec(memory_space=pltpu.VMEM)
    smem = pl.BlockSpec(memory_space=pltpu.SMEM)
    anywhere = pl.BlockSpec(memory_space=pl.ANY)
    single = jnp.float32

    def struct(*shape, dtype=jnp.float32):
        return jax.ShapeDtypeStruct(shape, dtype)

    stiffness = jnp.pad(degree_stiffness(count), (0, wide - count))[None]
    packed = jnp.concatenate([shapes, anchors.astype(jnp.float32)[:, :, None]], axis=2)
    packed = jnp.pad(packed.reshape(block, count + 1), ((0, 0), (0, wide - count - 1)))
    held = jnp.concatenate(
        [shifted(packed, 2), shifted(packed, 1), packed, shifted(packed, -1)], axis=0
    )
    place = held[:, count].astype(jnp.int32).reshape(slots, 3)
    held = jnp.where(jnp.arange(wide) < count, held, 0.0)
    ahead = jnp.mod(place[:, 0] - first_plane, total_planes)
    ahead = jnp.where(ahead > total_planes - BZ, ahead - total_planes, ahead)
    home = ((ahead >= 0) & (ahead < planes)).astype(jnp.int32)
    home = jnp.broadcast_to(home[:, None, None], (slots, parts, wide)).reshape(rows, wide)
    place = jnp.stack([ahead, place[:, 1], place[:, 2]], axis=1)

    spread_high, spread_low, synth_high, synth_low = pl.pallas_call(
        prepare_kernel,
        out_shape=[struct(points, spreading.shape[1], dtype=jnp.bfloat16)] * 2
        + [struct(points, wide, dtype=jnp.bfloat16)] * 2,
        in_specs=[vmem] * 2,
        out_specs=[vmem] * 4,
        compiler_params=pltpu.CompilerParams(vmem_limit_bytes=16 << 20),
        cost_estimate=pl.CostEstimate(flops=50_000_000, bytes_accessed=8 << 20, transcendentals=0),
        name="prepare",
    )(spreading, synthesis)

    def body(*refs):
        flow_kernel(devices, *refs)

    moments, result = pl.pallas_call(
        body,
        out_shape=[struct(10, planes, side, lanes), struct(block, wide)],
        in_specs=[smem, anywhere] + [vmem] * 7,
        out_specs=[anywhere, vmem],
        scratch_shapes=[
            pltpu.VMEM((10, planes, side, lanes), single),
            pltpu.VMEM((10, planes, side, lanes), single),
            pltpu.VMEM((3, planes, side, lanes), single),
            pltpu.VMEM((3, planes, side + BXY, lanes), single),
            pltpu.VMEM((18, side, lanes), single),
            pltpu.VMEM((BXY * rows, lanes), single),
            pltpu.VMEM((side, 2 * slots * BXY), jnp.bfloat16),
            pltpu.VMEM((2 * slots * BXY, 3 * planes * lanes), jnp.bfloat16),
            pltpu.VMEM((rows, wide), single),
            pltpu.VMEM((rows, wide), single),
            pltpu.VMEM((shared, wide), single),
            pltpu.VMEM((shared, wide), single),
            pltpu.VMEM((6, side, lanes), single),
            pltpu.VMEM((6, side, lanes), single),
            pltpu.VMEM((3, block, wide), single),
            pltpu.SemaphoreType.DMA((2,)),
            pltpu.SemaphoreType.DMA((7,)),
            pltpu.SemaphoreType.DMA((7,)),
        ],
        compiler_params=pltpu.CompilerParams(
            vmem_limit_bytes=VMEM_LIMIT, collective_id=0, has_side_effects=True
        ),
        name="flow",
    )(place, moments, held, home, stiffness, synth_high, synth_low, spread_high, spread_low)
    moments = pl.pallas_call(
        store_kernel,
        out_shape=struct(10, planes, side, lanes),
        in_specs=[anywhere],
        out_specs=anywhere,
        scratch_shapes=[pltpu.SemaphoreType.DMA((10,))],
        compiler_params=pltpu.CompilerParams(vmem_limit_bytes=1 << 20),
        name="store",
    )(moments)
    return moments, result[:, :count].reshape(owned, parts, count)


def solution(mesh):
    return jax.shard_map(
        per_device,
        mesh=mesh,
        in_specs=(P(None, "gz", None, None), P("gz", None, None), P("gz", None), P(), P()),
        out_specs=(P(None, "gz", None, None), P("gz", None, None)),
        check_vma=False,
    )
```
